32 devices in a mesh: loop: 8 (over z, x), rep: 4 (over y, core).
Axes of the slice: x: 2, y: 2, z: 4, core: 2. Of those that a mesh axis runs over, the one named last changes fastest.
Arguments:
- features: bfloat16 [8192, 512], P(('loop', 'rep')), may hold values from -6 to 6
- adj_values: bfloat16 [8, 64, 4, 128, 128], P('loop', 'rep'), may hold values from -0.125 to 0.125
- adj_rows: int32 [8, 64, 4], P('loop', 'rep'), may hold values from 0 to 7
- slot_counts: int32 [8, 64], P('loop', 'rep'), may hold values from 1 to 4, as said below
- w_self: bfloat16 [512, 512], replicated, may hold values from -0.1875 to 0.1875
- w_neigh: bfloat16 [512, 512], replicated, may hold values from -0.1875 to 0.1875
- cotangent: bfloat16 [8192, 512], P(('loop', 'rep')), may hold values from -6 to 6
Outputs:
- activations: bfloat16 [8192, 512], P(('loop', 'rep'))
- grad_features: bfloat16 [8192, 512], P(('loop', 'rep'))
- grad_self: float32 [512, 512], replicated
- grad_neigh: float32 [512, 512], replicated
The draws below stay inside these ranges and needn't reach their ends.
Inputs may be any that keep to these rules, and one draw needn't show every extreme that they name: `adj_rows`: A tile's rows lie in its own loop index's rows. Only the first slot_counts[l, c] slots of a column block are tiles of A; the others are ignored. The first column block of every device uses all 4 slots.
All inputs are finite; a program needn't handle non-finite values.
Results may differ from the reference program's by a relative error of at most 0.015.
Values may be sent and summed in bfloat16 or wider, within the bound.
A program may use at most 128 MiB of HBM per device.

```python
import math
import jax
import jax.numpy as jnp
from jax import lax

D = 512
TILE = 128
SLOTS = 4
ROWS_DEV = 256
NODES = 8192
COL_BLOCKS = 64
ROW_BLOCKS = 8
N_LOOP = 8
N_REP = 4


def draw_slot_counts(key, part):
    per_device = N_LOOP * (ROWS_DEV // TILE)
    counts = jax.random.randint(key, (N_LOOP, COL_BLOCKS), 1, SLOTS + 1).astype(jnp.int32)
    column = jnp.arange(COL_BLOCKS, dtype=jnp.int32)[None, :]
    return jnp.where(column % per_device == 0, SLOTS, counts).astype(jnp.int32)


def place_ends(values, own_key, least, top_value):
    longest = values.shape.index(max(values.shape))
    spots = []
    for shift in (0, 1):
        where = [jax.random.randint(jax.random.fold_in(own_key, axis), (), 0, length) for axis, length in enumerate(values.shape)]
        where[longest] = (where[longest] + shift) % values.shape[longest]
        spots.append(tuple(where))
    return values.at[spots[0]].set(least).at[spots[1]].set(top_value)


def shard_levels(stream_key, extent, shards, least, top_value):
    gain, own = 1.0, jax.random.fold_in(stream_key, 6)
    for position, parts in shards:
        steps = jnp.exp(jax.random.uniform(jax.random.fold_in(own, position), (parts,), jnp.float32, least / len(shards), top_value / len(shards)))
        gain = gain * jnp.repeat(steps, extent[position] // parts).reshape([-1 if axis == position else 1 for axis in range(len(extent))])
    return gain


def scatter_about(stream_key, dims, width, bound, cuts=(), kind=jnp.bfloat16):
    result = width * jax.random.normal(stream_key, dims, jnp.float32)
    if cuts:
        result = result * shard_levels(stream_key, dims, cuts, -0.22, 0.18)
    return jnp.clip(result, -bound, bound).astype(kind)


def setup_inputs(seed: int = 0) -> dict:
    seeds = jax.random.split(jax.random.key(seed), 8)
    return {
        "features": scatter_about(seeds[0], (NODES, D), 1.0, 6.0, ((0, 32),)),
        "adj_values": scatter_about(seeds[1], (N_LOOP, COL_BLOCKS, SLOTS, TILE, TILE), (TILE * N_LOOP * (SLOTS + 1) // 2) ** -0.5, 0.125, ((0, 8), (1, 4))),
        "adj_rows": place_ends(jax.random.randint(seeds[2], (N_LOOP, COL_BLOCKS, SLOTS), 0, ROW_BLOCKS), jax.random.fold_in(seeds[2], 1), 0, ROW_BLOCKS - 1).astype(jnp.int32),
        "slot_counts": draw_slot_counts(jax.random.fold_in(seeds[7], 71), 0),
        "w_self": scatter_about(seeds[4], (D, D), (2 * D) ** -0.5, 0.1875),
        "w_neigh": scatter_about(seeds[5], (D, D), (2 * D) ** -0.5, 0.1875),
        "cotangent": scatter_about(seeds[6], (NODES, D), 1.0, 6.0, ((0, 32),)),
    }


def reference(features, adj_values, adj_rows, slot_counts, w_self, w_neigh, cotangent):
    per_dev = ROWS_DEV // TILE
    cols_dev = N_LOOP * per_dev
    row_blocks = N_REP * per_dev
    columns = features.reshape(N_LOOP, N_REP, per_dev, TILE, D).transpose(1, 0, 2, 3, 4)
    columns = columns.reshape(N_REP, cols_dev, TILE, D)

    def masked(values, counts):
        live = jnp.arange(SLOTS, dtype=jnp.int32)[None, :] < counts[:, None]
        return values.astype(jnp.float32) * live.astype(jnp.float32)[:, :, None, None]

    def forward_shard(inputs):
        values, rows, counts = inputs
        values = values.reshape(N_REP, cols_dev, SLOTS, TILE, TILE)
        rows = rows.reshape(N_REP, cols_dev, SLOTS)
        counts = counts.reshape(N_REP, cols_dev)

        def step(total, group):
            vals, rws, cnts, block = group
            prod = jnp.einsum('csij,cjd->csid', masked(vals, cnts), block.astype(jnp.float32))
            return (total.at[rws.reshape(-1)].add(prod.reshape(-1, TILE, D)), None)
        start = jnp.zeros((row_blocks, TILE, D), jnp.float32)
        total, _ = lax.scan(step, start, (values, rows, counts, columns))
        return total.reshape(row_blocks * TILE, D)
    agg = lax.map(forward_shard, (adj_values, adj_rows, slot_counts)).reshape(NODES, D)
    hidden = agg.astype(jnp.bfloat16)
    z = jnp.dot(features, w_self, preferred_element_type=jnp.float32) + jnp.dot(hidden, w_neigh, preferred_element_type=jnp.float32)
    activations = jax.nn.silu(z).astype(jnp.bfloat16)
    sig = jax.nn.sigmoid(z)
    dz = (cotangent.astype(jnp.float32) * sig * (1.0 + z * (1.0 - sig))).astype(jnp.bfloat16)
    factor = 1.0 / math.sqrt(NODES)
    grad_self = jnp.dot(features.T, dz, preferred_element_type=jnp.float32) * factor
    grad_neigh = jnp.dot(hidden.T, dz, preferred_element_type=jnp.float32) * factor
    dagg = jnp.dot(dz, w_neigh.T, preferred_element_type=jnp.float32).astype(jnp.bfloat16)
    dagg_blocks = dagg.reshape(N_LOOP, row_blocks, TILE, D)

    def back_step(total, group):
        values, rows, counts, grads = group
        values = values.reshape(N_REP, cols_dev, SLOTS, TILE, TILE)
        rows = rows.reshape(N_REP, cols_dev, SLOTS)
        counts = counts.reshape(N_REP, cols_dev)

        def one_group(inner):
            vals, rws, cnts = inner
            picked = grads[rws].astype(jnp.float32)
            return jnp.einsum('csij,csid->cjd', masked(vals, cnts), picked)
        return (total + lax.map(one_group, (values, rows, counts)), None)
    start = jnp.zeros((N_REP, cols_dev, TILE, D), jnp.float32)
    colgrad, _ = lax.scan(back_step, start, (adj_values, adj_rows, slot_counts, dagg_blocks))
    colgrad = colgrad.reshape(N_REP, N_LOOP, per_dev, TILE, D).transpose(1, 0, 2, 3, 4).reshape(NODES, D)
    grad_features = (jnp.dot(dz, w_self.T, preferred_element_type=jnp.float32) + colgrad).astype(jnp.bfloat16)
    return (activations, grad_features, grad_self, grad_neigh)
```

```python
import functools
import math

import jax
import jax.numpy as jnp
from jax import lax
from jax.experimental import pallas as pl
from jax.experimental.pallas import tpu as pltpu
from jax.sharding import PartitionSpec as P

MESH = pl.DeviceIdType.MESH
SLAB_LIMIT = 8 * 1024 * 1024
OVER_ROWS = (((0,), (0,)), ((), ()))
OVER_COLS = (((1,), (1,)), ((), ()))


def mm(a, b, dims=(((1,), (0,)), ((), ()))):
    return lax.dot_general(a, b, dims, preferred_element_type=jnp.float32)


def loop(low, high, step):
    def one(k, carry):
        step(k)
        return carry

    lax.fori_loop(low, high, one, 0)


def kernel(
    nl, nr, scale,
    f_ref, adj_ref, rows_ref, cnt_ref, ws_ref, wn_ref, ct_ref,
    act_ref, gf_ref, gs_ref, gn_ref,
    dense, gat, acc, b1s, b1r, b2s, b2r, zf, fa, dz, dall,
    g1s, g1r, g32, g2s, g2r, g3f, g3s, g3r, gfin,
    f1s, f1r, f2s, f2r, total,
    sem_a, sem_x, rec_a, sem_b1, rec_b1, sem_b2, rec_b2, sem_d, sem_ds, rec_d,
    sem_g1, rec_g1, sem_g2, rec_g2, sem_g3, rec_g3, sem_g4, rec_g4, sem_g5, rec_g5,
    sem_g6, rec_g6, sem_f1, rec_f1, sem_f2, rec_f2,
):
    nz, ny = nl // 2, nr // 2
    rows, width = f_ref.shape
    tile = adj_ref.shape[-1]
    slots = adj_ref.shape[2]
    part = width // ny
    bf16, f32 = jnp.bfloat16, jnp.float32
    li, ri = lax.axis_index("loop"), lax.axis_index("rep")
    z, x = lax.div(li, 2), lax.rem(li, 2)
    y, c = lax.div(ri, 2), lax.rem(ri, 2)
    xp = z * 2 + 1 - x
    sib = y * 2 + 1 - c

    def zat(k):
        return lax.rem(z + k, nz)

    def yat(k):
        return lax.rem(y + k, ny)

    def lat(k):
        return lax.rem(li + k, nl)

    def rowsof(r):
        return pl.ds(pl.multiple_of(r * rows, rows), rows)

    def send(src, dst, s, r, lo, re):
        return pltpu.make_async_remote_copy(
            src_ref=src, dst_ref=dst, send_sem=s, recv_sem=r,
            device_id=(lo, re), device_id_type=MESH,
        )

    barrier = pltpu.get_barrier_semaphore()
    for k in range(1, nl):
        pl.semaphore_signal(barrier, inc=1, device_id=(lat(k), ri), device_id_type=MESH)
    for k in range(1, ny):
        pl.semaphore_signal(
            barrier, inc=1, device_id=(li, yat(k) * 2 + c), device_id_type=MESH
        )
    pl.semaphore_signal(barrier, inc=1, device_id=(li, sib), device_id_type=MESH)
    pl.semaphore_wait(barrier, nl - 1 + ny)

    def send_a(k):
        return send(f_ref, gat.at[li], sem_a.at[k], rec_a.at[li], zat(k) * 2 + x, ri)

    def send_x0():
        return send(f_ref, gat.at[li], sem_x.at[0], rec_a.at[li], xp, ri)

    def send_x(k):
        j = zat(k) * 2 + x
        return send(gat.at[j], gat.at[j], sem_x.at[k], rec_a.at[j], xp, ri)

    def got_a(j):
        send(gat.at[j], gat.at[j], sem_x.at[0], rec_a.at[j], xp, ri).wait_recv()

    send_x0().start()
    for k in range(1, nz):
        send_a(k).start()

    per = rows // tile
    row_blocks = nr * per

    def build(col):
        j, h = lax.div(col, per), lax.rem(col, per)
        cols = pl.ds(pl.multiple_of(h * tile, tile), tile)
        count = cnt_ref[0, col]
        places = [
            jnp.where(s < count, rows_ref[0, col, s], -1) for s in range(slots)
        ]

        for b in range(row_blocks):
            block = jnp.zeros((tile, tile), f32)
            for s in range(slots):
                keep = jnp.where(places[s] == b, 1.0, 0.0).astype(f32)
                block = block + adj_ref[0, col, s].astype(f32) * keep
            dense[j, b * tile : (b + 1) * tile, cols] = block.astype(bf16)

    loop(0, nl * per, build)
    zf[...] = mm(f_ref[...], ws_ref[...])
    fa[0] = f_ref[...]
    acc[...] = mm(dense[li], f_ref[...])

    def column(k):
        j = zat(k) * 2 + x
        got_a(j)
        send_x(k).start()
        acc[...] += mm(dense[j], gat[j])

    loop(1, nz, column)

    def across(k):
        j = zat(k) * 2 + 1 - x
        got_a(j)
        acc[...] += mm(dense[j], gat[j])

    loop(0, nz, across)

    def send_b1(k):
        return send(b1s.at[k], b1r.at[k], sem_b1.at[k], rec_b1.at[k], li, sib)

    def send_b2(k):
        return send(
            b2s.at[k - 1], b2r.at[k - 1], sem_b2.at[k - 1], rec_b2.at[k - 1],
            li, yat(k) * 2 + c,
        )

    order = list(range(1, ny)) + [0]
    for k in order:
        b1s[k] = acc[rowsof(yat(k) * 2 + 1 - c), :].astype(bf16)
        send_b1(k).start()
    for k in order:
        send_b1(k).wait_recv()
        summed = acc[rowsof(yat(k) * 2 + c), :] + b1r[k].astype(f32)
        if k:
            b2s[k - 1] = summed.astype(bf16)
            send_b2(k).start()
        else:
            total[...] = summed
    for k in range(1, ny):
        send_b2(k).wait_recv()
        total[...] += b2r[k - 1].astype(f32)
    fa[1] = total[...].astype(bf16)

    zz = zf[...] + mm(fa[1], wn_ref[...])
    sig = jax.nn.sigmoid(zz)
    act_ref[...] = (zz * sig).astype(bf16)
    dz[...] = (ct_ref[...].astype(f32) * sig * (1.0 + zz * (1.0 - sig))).astype(bf16)
    dall[rowsof(ri), :] = mm(dz[...], wn_ref[...], OVER_COLS).astype(bf16)

    def send_d(k):
        at = dall.at[rowsof(ri)]
        return send(at, at, sem_d.at[k - 1], rec_d.at[ri], li, yat(k) * 2 + c)

    def send_ds(k):
        r = yat(k) * 2 + c
        at = dall.at[rowsof(r)]
        return send(at, at, sem_ds.at[k], rec_d.at[r], li, sib)

    def got_d(r):
        at = dall.at[rowsof(r)]
        send(at, at, sem_ds.at[0], rec_d.at[r], li, sib).wait_recv()

    for k in range(1, ny):
        send_d(k).start()
    send_ds(0).start()

    send_g1 = send(g1s, g1r, sem_g1, rec_g1, li, sib)
    g1s[...] = mm(fa[1 - c], dz[...], OVER_ROWS).astype(bf16)
    send_g1.start()
    g32[...] = mm(fa[c], dz[...], OVER_ROWS)
    for k in range(1, ny):
        got_d(yat(k) * 2 + c)
        send_ds(k).start()
    send_g1.wait_recv()
    g32[...] += g1r[...].astype(f32)

    def partof(yy):
        return pl.ds(pl.multiple_of(yy * part, part), part)

    def send_g2(k):
        return send(
            g2s.at[k - 1], g2r.at[k - 1], sem_g2.at[k - 1], rec_g2.at[k - 1],
            li, yat(k) * 2 + c,
        )

    for k in range(1, ny):
        g2s[k - 1] = g32[partof(yat(k)), :].astype(bf16)
        send_g2(k).start()
    for k in range(ny):
        got_d(yat(k) * 2 + 1 - c)

    def send_f1(k):
        return send(f1s.at[k], f1r.at[k], sem_f1.at[k], rec_f1.at[k], xp, ri)

    def send_f2(k):
        return send(
            f2s.at[k - 1], f2r.at[k - 1], sem_f2.at[k - 1], rec_f2.at[k - 1],
            zat(k) * 2 + x, ri,
        )

    def away(i):
        k = lax.rem(i, nz)
        f1s[k] = mm(dense[zat(k) * 2 + 1 - x], dall[...], OVER_ROWS).astype(bf16)
        send_f1(k).start()

    loop(1, nz + 1, away)

    def send_g3(k):
        return send(
            g3s.at[lat(k)], g3r.at[k - 1], sem_g3.at[k - 1], rec_g3.at[k - 1], lat(k), ri
        )

    mine = g32[partof(y), :]
    for k in range(1, ny):
        send_g2(k).wait_recv()
        mine = mine + g2r[k - 1].astype(f32)
    g3f[...] = mine.reshape(g3f.shape)
    g3s[...] = g3f[...].astype(bf16)
    for k in range(1, nl):
        send_g3(k).start()

    def home(k):
        value = mm(dense[zat(k) * 2 + x], dall[...], OVER_ROWS)
        send_f1(k).wait_recv()
        f2s[k - 1] = (value + f1r[k].astype(f32)).astype(bf16)
        send_f2(k).start()

    loop(1, nz, home)

    def send_g4(k):
        at = gfin.at[c, y, li]
        return send(at, at, sem_g4.at[k - 1], rec_g4.at[li], lat(k), ri)

    small = g3f[li]
    for k in range(1, nl):
        send_g3(k).wait_recv()
        small = small + g3r[k - 1].astype(f32)
    gfin[c, y, li] = small.astype(bf16)
    for k in range(1, nl):
        send_g4(k).start()
    total[...] = mm(dz[...], ws_ref[...], OVER_COLS) + mm(
        dense[li], dall[...], OVER_ROWS
    )
    send_f1(0).wait_recv()
    total[...] += f1r[0].astype(f32)
    for k in range(1, nl):
        at = gfin.at[c, y, lat(k)]
        send(at, at, sem_g4.at[0], rec_g4.at[lat(k)], lat(k), ri).wait_recv()

    def send_g5(k):
        at = gfin.at[c, y]
        return send(at, at, sem_g5.at[k - 1], rec_g5.at[y], li, yat(k) * 2 + c)

    def send_g6(k):
        at = gfin.at[c, yat(k)]
        return send(at, at, sem_g6.at[k], rec_g6.at[yat(k)], li, sib)

    for k in range(1, ny):
        send_g5(k).start()
    send_g6(0).start()
    for k in range(1, ny):
        at = gfin.at[c, yat(k)]
        send(at, at, sem_g5.at[0], rec_g5.at[yat(k)], li, yat(k) * 2 + c).wait_recv()
        send_g6(k).start()
    for k in range(1, nz):
        send_f2(k).wait_recv()
        total[...] += f2r[k - 1].astype(f32)
    gf_ref[...] = total[...].astype(bf16)
    for k in range(ny):
        at = gfin.at[1 - c, yat(k)]
        send(at, at, sem_g6.at[0], rec_g6.at[yat(k)], li, sib).wait_recv()
    gs_ref[...] = gfin[0].reshape(width, width).astype(f32) * scale
    gn_ref[...] = gfin[1].reshape(width, width).astype(f32) * scale

    send_x0().wait_send()
    for k in range(1, nz):
        send_a(k).wait_send()
        send_x(k).wait_send()
        send_f2(k).wait_send()
    for k in range(nz):
        send_f1(k).wait_send()
    for k in range(ny):
        send_b1(k).wait_send()
        send_ds(k).wait_send()
        send_g6(k).wait_send()
    for k in range(1, ny):
        send_b2(k).wait_send()
        send_d(k).wait_send()
        send_g2(k).wait_send()
        send_g5(k).wait_send()
    send_g1.wait_send()
    for k in range(1, nl):
        send_g3(k).wait_send()
        send_g4(k).wait_send()


def fused(nl, nr, features, adj_values, adj_rows, slot_counts, w_self, w_neigh, cotangent):
    rows, width = features.shape
    bf16, f32 = jnp.bfloat16, jnp.float32
    nz, ny = nl // 2, nr // 2
    part = width // ny
    q = part // nl
    scale = 1.0 / math.sqrt(rows * nl * nr)
    vm = pl.BlockSpec(memory_space=pltpu.VMEM)
    sm = pl.BlockSpec(memory_space=pltpu.SMEM)

    def buf(*shape):
        return pltpu.VMEM(shape, bf16)

    def wide(*shape):
        return pltpu.VMEM(shape, f32)

    def dma(*shape):
        return pltpu.SemaphoreType.DMA(shape)

    out = pl.pallas_call(
        functools.partial(kernel, nl, nr, scale),
        out_shape=(
            jax.ShapeDtypeStruct((rows, width), bf16),
            jax.ShapeDtypeStruct((rows, width), bf16),
            jax.ShapeDtypeStruct((width, width), f32),
            jax.ShapeDtypeStruct((width, width), f32),
        ),
        in_specs=[vm, vm, sm, sm, vm, vm, vm],
        out_specs=(vm, vm, vm, vm),
        scratch_shapes=[
            buf(nl, nr * rows, rows), buf(nl, rows, width), wide(nr * rows, width),
            buf(ny, rows, width), buf(ny, rows, width),
            buf(ny - 1, rows, width), buf(ny - 1, rows, width),
            wide(rows, width), buf(2, rows, width), buf(rows, width), buf(nr * rows, width),
            buf(width, width), buf(width, width), wide(width, width),
            buf(ny - 1, part, width), buf(ny - 1, part, width),
            wide(nl, q, width), buf(nl, q, width), buf(nl - 1, q, width),
            buf(2, ny, nl, q, width),
            buf(nz, rows, width), buf(nz, rows, width),
            buf(nz - 1, rows, width), buf(nz - 1, rows, width), wide(rows, width),
            dma(nz), dma(nz), dma(nl), dma(ny), dma(ny), dma(ny - 1), dma(ny - 1),
            dma(ny - 1), dma(ny), dma(nr),
            pltpu.SemaphoreType.DMA, pltpu.SemaphoreType.DMA, dma(ny - 1), dma(ny - 1),
            dma(nl - 1), dma(nl - 1), dma(nl - 1), dma(nl), dma(ny - 1), dma(ny),
            dma(ny), dma(ny), dma(nz), dma(nz), dma(nz - 1), dma(nz - 1),
        ],
        compiler_params=pltpu.CompilerParams(
            collective_id=0, has_side_effects=True, vmem_limit_bytes=48 * 1024 * 1024
        ),
    )(features, adj_values, adj_rows, slot_counts, w_self, w_neigh, cotangent)
    return tuple(out)


def choose(nl, nr, features, *rest):
    rows = features.shape[0]
    if nl * nr * rows * rows * 2 > SLAB_LIMIT:
        return body(features, *rest)
    return fused(nl, nr, features, *rest)


def body(features, adj_values, adj_rows, slot_counts, w_self, w_neigh, cotangent):
    rows_dev, width = features.shape
    tile = adj_values.shape[-1]
    nodes = rows_dev * lax.axis_size("loop") * lax.axis_size("rep")
    row_blocks = lax.axis_size("rep") * rows_dev // tile
    live = lax.broadcasted_iota(jnp.int32, adj_rows.shape[1:], 1) < slot_counts[0][:, None]
    tiles_live = adj_values[0] * live.astype(jnp.bfloat16)[:, :, None, None]
    block_rows = adj_rows[0]

    def tiles_for(count):
        blocks = count // tile
        return (tiles_live, block_rows)

    start_rows = jnp.zeros((row_blocks, tile, width), jnp.float32)
    piece = lax.all_gather(features, "loop", axis=0, tiled=True)
    blocks = piece.shape[0] // tile
    picked, targets = tiles_for(piece.shape[0])
    prod = jnp.einsum(
        "csij,cjd->csid",
        picked,
        piece.reshape(blocks, tile, width),
        preferred_element_type=jnp.float32,
    )
    partial_rows = start_rows.at[targets.reshape(-1)].add(prod.reshape(-1, tile, width))
    partial_flat = partial_rows.reshape(row_blocks * tile, width)
    agg = lax.psum_scatter(
        partial_flat.astype(jnp.bfloat16), "rep", scatter_dimension=0, tiled=True
    )
    z = jnp.dot(features, w_self, preferred_element_type=jnp.float32) + jnp.dot(
        agg, w_neigh, preferred_element_type=jnp.float32
    )
    activations = jax.nn.silu(z).astype(jnp.bfloat16)
    sig = jax.nn.sigmoid(z)
    dz = (cotangent.astype(jnp.float32) * sig * (1.0 + z * (1.0 - sig))).astype(jnp.bfloat16)
    over_rows = (((0,), (0,)), ((), ()))
    over_cols = (((1,), (1,)), ((), ()))
    dagg = lax.dot_general(dz, w_neigh, over_cols, preferred_element_type=jnp.float32).astype(
        jnp.bfloat16
    )
    dagg_rows = lax.all_gather(dagg, "rep", axis=0, tiled=True)
    dagg_blocks = dagg_rows.reshape(row_blocks, tile, width)
    count = lax.axis_size("loop") * rows_dev
    picked, targets = tiles_for(count)
    grads = dagg_blocks[targets]
    neighbour_part = lax.psum_scatter(
        jnp.einsum("csij,csid->cjd", picked, grads, preferred_element_type=jnp.float32)
        .reshape(count, width)
        .astype(jnp.bfloat16),
        "loop",
        scatter_dimension=0,
        tiled=True,
    ).astype(jnp.float32)
    local_self = lax.dot_general(features, dz, over_rows, preferred_element_type=jnp.float32)
    local_neigh = lax.dot_general(agg, dz, over_rows, preferred_element_type=jnp.float32)
    sums = lax.psum((local_self, local_neigh), ("loop", "rep"))
    factor = 1.0 / math.sqrt(nodes)
    self_part = lax.dot_general(dz, w_self, over_cols, preferred_element_type=jnp.float32)
    grad_features = (self_part + neighbour_part).astype(jnp.bfloat16)
    return (activations, grad_features, sums[0] * factor, sums[1] * factor)


def solution(mesh):
    placed = (
        P(("loop", "rep"), None),
        P("loop", "rep", None, None, None),
        P("loop", "rep", None),
        P("loop", "rep"),
        P(),
        P(),
        P(("loop", "rep"), None),
    )
    return jax.shard_map(
        functools.partial(choose, mesh.shape["loop"], mesh.shape["rep"]),
        mesh=mesh,
        in_specs=placed,
        out_specs=(P(("loop", "rep"), None), P(("loop", "rep"), None), P(), P()),
        check_vma=False,
    )
```

```python
import functools
import math

import jax
import jax.numpy as jnp
from jax import lax
from jax.experimental import pallas as pl
from jax.experimental.pallas import tpu as pltpu
from jax.sharding import PartitionSpec as P

MESH = pl.DeviceIdType.MESH
HALVES = 2
SLAB_LIMIT = 8 * 1024 * 1024
OVER_ROWS = (((0,), (0,)), ((), ()))
OVER_COLS = (((1,), (1,)), ((), ()))


def mm(a, b, dims=(((1,), (0,)), ((), ()))):
    return lax.dot_general(a, b, dims, preferred_element_type=jnp.float32)


def loop(low, high, step):
    def one(k, carry):
        step(k)
        return carry

    lax.fori_loop(low, high, one, 0)


def kernel(
    nl, nr,
    f_hbm, adj_hbm, rows_ref, cnt_ref, ws_hbm, wn_hbm, ct_hbm,
    act_ref, gf_ref, gs_ref, gn_ref,
    f_ref, adj_ref, ws_ref, wn_ref, ct_ref, sem_in,
    dense, gat, acc, b1s, b1r, b2s, b2r, zf, fa, dz, dall,
    g1s, g1r, g32, g2s, g2r, g3f, g3s, g3r, gfin,
    f1s, f1r, ups, upr, dns, dnr, value, total,
    sem_au, sem_ad, sem_x, rec_a, sem_b1, rec_b1, sem_b2, rec_b2, sem_d, sem_ds, rec_d,
    sem_g1, rec_g1, sem_g2, rec_g2, sem_g3, rec_g3, sem_g4, rec_g4, sem_g5, rec_g5,
    sem_g6, rec_g6, sem_f1, rec_f1, sem_up, rec_up, sem_dn, rec_dn,
):
    nz, ny = nl // 2, nr // 2
    rows, width = f_ref.shape
    tile = adj_ref.shape[-1]
    slots = adj_ref.shape[2]
    half = rows // HALVES
    part = width // ny
    bf16, f32 = jnp.bfloat16, jnp.float32
    li, ri = lax.axis_index("loop"), lax.axis_index("rep")
    z, x = lax.div(li, 2), lax.rem(li, 2)
    y, c = lax.div(ri, 2), lax.rem(ri, 2)
    xp = z * 2 + 1 - x
    sib = y * 2 + 1 - c
    below, above = z > 0, z < nz - 1

    def zat(k):
        return lax.rem(z + k, nz)

    def yat(k):
        return lax.rem(y + k, ny)

    def lat(k):
        return lax.rem(li + k, nl)

    def rowsof(r):
        return pl.ds(pl.multiple_of(r * rows, rows), rows)

    def send(src, dst, s, r, lo, re):
        return pltpu.make_async_remote_copy(
            src_ref=src, dst_ref=dst, send_sem=s, recv_sem=r,
            device_id=(lo, re), device_id_type=MESH,
        )

    barrier = pltpu.get_barrier_semaphore()
    for k in range(1, nl):
        pl.semaphore_signal(barrier, inc=1, device_id=(lat(k), ri), device_id_type=MESH)
    for k in range(1, ny):
        pl.semaphore_signal(
            barrier, inc=1, device_id=(li, yat(k) * 2 + c), device_id_type=MESH
        )
    pl.semaphore_signal(barrier, inc=1, device_id=(li, sib), device_id_type=MESH)
    loads = [
        pltpu.make_async_copy(src, dst, sem_in.at[i])
        for i, (src, dst) in enumerate(
            ((f_hbm, f_ref), (adj_hbm, adj_ref), (ws_hbm, ws_ref), (wn_hbm, wn_ref), (ct_hbm, ct_ref))
        )
    ]
    for load in loads:
        load.start()
    loads[0].wait()
    pl.semaphore_wait(barrier, nl - 1 + ny)

    def block(p, h):
        at = pl.ds(h * half, half)
        return gat.at[p * 2 + x, at, :]

    def own(h):
        return f_ref.at[pl.ds(h * half, half), :]

    def send_x(p, h, src=None):
        at = block(p, h)
        return send(
            at if src is None else src, at, sem_x.at[p, h], rec_a.at[p * 2 + x, h], xp, ri
        )

    def send_au(p, h, src=None):
        at = block(p, h)
        return send(
            at if src is None else src, at, sem_au.at[p, h], rec_a.at[p * 2 + x, h],
            (z + 1) * 2 + x, ri,
        )

    def send_ad(p, h, src=None):
        at = block(p, h)
        return send(
            at if src is None else src, at, sem_ad.at[p, h], rec_a.at[p * 2 + x, h],
            (z - 1) * 2 + x, ri,
        )

    def got_a(j, h):
        at = gat.at[j, pl.ds(h * half, half), :]
        send(at, at, sem_x.at[0, 0], rec_a.at[j, h], xp, ri).wait_recv()

    for h in range(HALVES):
        @pl.when(above)
        def _():
            send_au(z, h, own(h)).start()

        @pl.when(below)
        def _():
            send_ad(z, h, own(h)).start()

        send_x(z, h, own(h)).start()

    for load in loads[1:]:
        load.wait()
    per = rows // tile
    row_blocks = nr * per

    def build(col):
        j, h = lax.div(col, per), lax.rem(col, per)
        cols = pl.ds(pl.multiple_of(h * tile, tile), tile)
        count = cnt_ref[0, col]
        places = [
            jnp.where(s < count, rows_ref[0, s, col], -1) for s in range(slots)
        ]

        for b in range(row_blocks):
            summed = jnp.zeros((tile, tile), f32)
            for s in range(slots):
                keep = jnp.where(places[s] == b, 1.0, 0.0).astype(f32)
                summed = summed + adj_ref[0, col, s].astype(f32) * keep
            dense[j, b * tile : (b + 1) * tile, cols] = summed.astype(bf16)

    loop(0, nl * per, build)
    zf[...] = mm(f_ref[...], ws_ref[...])
    fa[0] = f_ref[...]
    acc[...] = mm(dense[li], f_ref[...])

    for k in range(1, nz):
        for h in range(HALVES):
            @pl.when(z >= k)
            def _():
                got_a((z - k) * 2 + x, h)

                @pl.when(above)
                def _():
                    send_au(z - k, h).start()

                send_x(z - k, h).start()

            @pl.when(z + k < nz)
            def _():
                got_a((z + k) * 2 + x, h)

                @pl.when(below)
                def _():
                    send_ad(z + k, h).start()

                send_x(z + k, h).start()

    def column(k):
        j = zat(k) * 2 + x
        acc[...] += mm(dense[j], gat[j])

    loop(1, nz, column)

    def across(k):
        j = zat(k) * 2 + 1 - x
        for h in range(HALVES):
            got_a(j, h)
        acc[...] += mm(dense[j], gat[j])

    loop(0, nz, across)

    def send_b1(k):
        return send(b1s.at[k], b1r.at[k], sem_b1.at[k], rec_b1.at[k], li, sib)

    def send_b2(k):
        return send(
            b2s.at[k - 1], b2r.at[k - 1], sem_b2.at[k - 1], rec_b2.at[k - 1],
            li, yat(k) * 2 + c,
        )

    order = list(range(1, ny)) + [0]
    for k in order:
        b1s[k] = acc[rowsof(yat(k) * 2 + 1 - c), :].astype(bf16)
        send_b1(k).start()
    for k in order:
        send_b1(k).wait_recv()
        summed = acc[rowsof(yat(k) * 2 + c), :] + b1r[k].astype(f32)
        if k:
            b2s[k - 1] = summed.astype(bf16)
            send_b2(k).start()
        else:
            total[...] = summed
    for k in range(1, ny):
        send_b2(k).wait_recv()
        total[...] += b2r[k - 1].astype(f32)
    fa[1] = total[...].astype(bf16)

    zz = zf[...] + mm(fa[1], wn_ref[...])
    sig = jax.nn.sigmoid(zz)
    act_ref[...] = (zz * sig).astype(bf16)
    dz[...] = (ct_ref[...].astype(f32) * sig * (1.0 + zz * (1.0 - sig))).astype(bf16)
    dall[rowsof(ri), :] = mm(dz[...], wn_ref[...], OVER_COLS).astype(bf16)

    def send_d(k):
        at = dall.at[rowsof(ri)]
        return send(at, at, sem_d.at[k - 1], rec_d.at[ri], li, yat(k) * 2 + c)

    def send_ds(k):
        r = yat(k) * 2 + c
        at = dall.at[rowsof(r)]
        return send(at, at, sem_ds.at[k], rec_d.at[r], li, sib)

    def got_d(r):
        at = dall.at[rowsof(r)]
        send(at, at, sem_ds.at[0], rec_d.at[r], li, sib).wait_recv()

    for k in range(1, ny):
        send_d(k).start()
    send_ds(0).start()

    send_g1 = send(g1s, g1r, sem_g1, rec_g1, li, sib)
    g1s[...] = mm(fa[1 - c], dz[...], OVER_ROWS).astype(bf16)
    send_g1.start()
    g32[...] = mm(fa[c], dz[...], OVER_ROWS)
    for k in range(1, ny):
        got_d(yat(k) * 2 + c)
        send_ds(k).start()
    send_g1.wait_recv()
    g32[...] += g1r[...].astype(f32)

    def partof(yy):
        return pl.ds(pl.multiple_of(yy * part, part), part)

    def send_g2(k):
        return send(
            g2s.at[k - 1], g2r.at[k - 1], sem_g2.at[k - 1], rec_g2.at[k - 1],
            li, yat(k) * 2 + c,
        )

    for k in range(1, ny):
        g2s[k - 1] = g32[partof(yat(k)), :].astype(bf16)
        send_g2(k).start()
    for k in range(ny):
        got_d(yat(k) * 2 + 1 - c)

    def send_f1(d, h):
        return send(f1s.at[d, h], f1r.at[d, h], sem_f1.at[d, h], rec_f1.at[d, h], xp, ri)

    def send_up(d, h):
        return send(
            ups.at[d, h], upr.at[d, h], sem_up.at[d, h], rec_up.at[d, h], (z + 1) * 2 + x, ri
        )

    def send_dn(d, h):
        return send(
            dns.at[d, h], dnr.at[d, h], sem_dn.at[d, h], rec_dn.at[d, h], (z - 1) * 2 + x, ri
        )

    def away(d):
        product = mm(dense[d * 2 + 1 - x], dall[...], OVER_ROWS).astype(bf16)
        f1s[d] = product.reshape(HALVES, half, width)
        for h in range(HALVES):
            send_f1(d, h).start()

    def home(d, move, out, come, more):
        product = mm(dense[d * 2 + x], dall[...], OVER_ROWS)
        value[...] = product.reshape(HALVES, half, width)
        for h in range(HALVES):
            send_f1(d, h).wait_recv()
            value[h] += f1r[d, h].astype(f32)

            @pl.when(more)
            def _():
                move(d, h).wait_recv()
                value[h] += come[d, h].astype(f32)

            out[d, h] = value[h].astype(bf16)
            move(d, h).start()

    def sides(k, up, down):
        @pl.when(z + k < nz)
        def _():
            up(z + k)

        @pl.when(z >= k)
        def _():
            down(z - k)

    for k in range(nz - 1, nz // 2 - 1, -1):
        sides(k, away, away)

    def send_g3(k):
        return send(
            g3s.at[lat(k)], g3r.at[k - 1], sem_g3.at[k - 1], rec_g3.at[k - 1], lat(k), ri
        )

    mine = g32[partof(y), :]
    for k in range(1, ny):
        send_g2(k).wait_recv()
        mine = mine + g2r[k - 1].astype(f32)
    g3f[...] = mine.reshape(g3f.shape)
    g3s[...] = g3f[...].astype(bf16)
    for k in range(1, nl):
        send_g3(k).start()

    for k in range(nz // 2 - 1, 0, -1):
        sides(k, away, away)
    away(z)

    def home_up(d):
        home(d, send_up, ups, upr, below)

    def home_down(d):
        home(d, send_dn, dns, dnr, above)

    for k in range(nz - 1, nz // 2 - 1, -1):
        sides(k, home_up, home_down)

    def send_g4(k):
        at = gfin.at[c, y, li]
        return send(at, at, sem_g4.at[k - 1], rec_g4.at[li], lat(k), ri)

    small = g3f[li]
    for k in range(1, nl):
        send_g3(k).wait_recv()
        small = small + g3r[k - 1].astype(f32)
    gfin[c, y, li] = small.astype(bf16)
    for k in range(1, nl):
        send_g4(k).start()
    for k in range(nz // 2 - 1, 0, -1):
        sides(k, home_up, home_down)
    total[...] = mm(dz[...], ws_ref[...], OVER_COLS) + mm(
        dense[li], dall[...], OVER_ROWS
    )
    for k in range(1, nl):
        at = gfin.at[c, y, lat(k)]
        send(at, at, sem_g4.at[0], rec_g4.at[lat(k)], lat(k), ri).wait_recv()

    def send_g5(k):
        at = gfin.at[c, y]
        return send(at, at, sem_g5.at[k - 1], rec_g5.at[y], li, yat(k) * 2 + c)

    def send_g6(k):
        at = gfin.at[c, yat(k)]
        return send(at, at, sem_g6.at[k], rec_g6.at[yat(k)], li, sib)

    for k in range(1, ny):
        send_g5(k).start()
    send_g6(0).start()
    for k in range(1, ny):
        at = gfin.at[c, yat(k)]
        send(at, at, sem_g5.at[0], rec_g5.at[yat(k)], li, yat(k) * 2 + c).wait_recv()
        send_g6(k).start()
    for h in range(HALVES):
        at = slice(h * half, (h + 1) * half)
        send_f1(z, h).wait_recv()
        total[at] += f1r[z, h].astype(f32)

        @pl.when(below)
        def _():
            send_up(z, h).wait_recv()
            total[at] += upr[z, h].astype(f32)

        @pl.when(above)
        def _():
            send_dn(z, h).wait_recv()
            total[at] += dnr[z, h].astype(f32)

    gf_ref[...] = total[...].astype(bf16)
    for k in range(ny):
        at = gfin.at[1 - c, yat(k)]
        send(at, at, sem_g6.at[0], rec_g6.at[yat(k)], li, sib).wait_recv()
    gs_ref[...] = gfin[0].reshape(width, width)
    gn_ref[...] = gfin[1].reshape(width, width)

    for h in range(HALVES):
        for p in range(nz):
            send_x(p, h).wait_send()
            send_f1(p, h).wait_send()

            @pl.when(above & (p <= z))
            def _():
                send_au(p, h).wait_send()

            @pl.when(below & (p >= z))
            def _():
                send_ad(p, h).wait_send()

            @pl.when(p > z)
            def _():
                send_up(p, h).wait_send()

            @pl.when(p < z)
            def _():
                send_dn(p, h).wait_send()

    for k in range(ny):
        send_b1(k).wait_send()
        send_ds(k).wait_send()
        send_g6(k).wait_send()
    for k in range(1, ny):
        send_b2(k).wait_send()
        send_d(k).wait_send()
        send_g2(k).wait_send()
        send_g5(k).wait_send()
    send_g1.wait_send()
    for k in range(1, nl):
        send_g3(k).wait_send()
        send_g4(k).wait_send()


def fused(nl, nr, features, adj_values, adj_rows, slot_counts, w_self, w_neigh, cotangent):
    rows, width = features.shape
    bf16, f32 = jnp.bfloat16, jnp.float32
    nz, ny = nl // 2, nr // 2
    part = width // ny
    q = part // nl
    scale = 1.0 / math.sqrt(rows * nl * nr)
    vm = pl.BlockSpec(memory_space=pltpu.VMEM)
    sm = pl.BlockSpec(memory_space=pltpu.SMEM)
    hbm = pl.BlockSpec(memory_space=pl.ANY)
    half = rows // HALVES

    def buf(*shape):
        return pltpu.VMEM(shape, bf16)

    def wide(*shape):
        return pltpu.VMEM(shape, f32)

    def dma(*shape):
        return pltpu.SemaphoreType.DMA(shape)

    out = pl.pallas_call(
        functools.partial(kernel, nl, nr),
        out_shape=(
            jax.ShapeDtypeStruct((rows, width), bf16),
            jax.ShapeDtypeStruct((rows, width), bf16),
            jax.ShapeDtypeStruct((width, width), bf16),
            jax.ShapeDtypeStruct((width, width), bf16),
        ),
        in_specs=[hbm, hbm, sm, sm, hbm, hbm, hbm],
        out_specs=(vm, vm, vm, vm),
        scratch_shapes=[
            buf(rows, width), buf(*adj_values.shape), buf(width, width), buf(width, width),
            buf(rows, width), dma(5),
            buf(nl, nr * rows, rows), buf(nl, rows, width), wide(nr * rows, width),
            buf(ny, rows, width), buf(ny, rows, width),
            buf(ny - 1, rows, width), buf(ny - 1, rows, width),
            wide(rows, width), buf(2, rows, width), buf(rows, width), buf(nr * rows, width),
            buf(width, width), buf(width, width), wide(width, width),
            buf(ny - 1, part, width), buf(ny - 1, part, width),
            wide(nl, q, width), buf(nl, q, width), buf(nl - 1, q, width),
            buf(2, ny, nl, q, width),
            *[buf(nz, HALVES, half, width) for _ in range(6)],
            wide(HALVES, half, width), wide(rows, width),
            dma(nz, HALVES), dma(nz, HALVES), dma(nz, HALVES), dma(nl, HALVES), dma(ny), dma(ny), dma(ny - 1), dma(ny - 1),
            dma(ny - 1), dma(ny), dma(nr),
            pltpu.SemaphoreType.DMA, pltpu.SemaphoreType.DMA, dma(ny - 1), dma(ny - 1),
            dma(nl - 1), dma(nl - 1), dma(nl - 1), dma(nl), dma(ny - 1), dma(ny),
            dma(ny), dma(ny), *[dma(nz, HALVES) for _ in range(6)],
        ],
        compiler_params=pltpu.CompilerParams(
            collective_id=0, has_side_effects=True, vmem_limit_bytes=60 * 1024 * 1024
        ),
    )(features, adj_values, jnp.swapaxes(adj_rows, 1, 2), slot_counts, w_self, w_neigh, cotangent)
    return (out[0], out[1], out[2].astype(f32) * scale, out[3].astype(f32) * scale)


def choose(nl, nr, features, *rest):
    rows = features.shape[0]
    if nl * nr * rows * rows * 2 > SLAB_LIMIT:
        return body(features, *rest)
    return fused(nl, nr, features, *rest)


def body(features, adj_values, adj_rows, slot_counts, w_self, w_neigh, cotangent):
    rows_dev, width = features.shape
    tile = adj_values.shape[-1]
    nodes = rows_dev * lax.axis_size("loop") * lax.axis_size("rep")
    row_blocks = lax.axis_size("rep") * rows_dev // tile
    live = lax.broadcasted_iota(jnp.int32, adj_rows.shape[1:], 1) < slot_counts[0][:, None]
    tiles_live = adj_values[0] * live.astype(jnp.bfloat16)[:, :, None, None]
    block_rows = adj_rows[0]

    def tiles_for(count):
        blocks = count // tile
        return (tiles_live, block_rows)

    start_rows = jnp.zeros((row_blocks, tile, width), jnp.float32)
    piece = lax.all_gather(features, "loop", axis=0, tiled=True)
    blocks = piece.shape[0] // tile
    picked, targets = tiles_for(piece.shape[0])
    prod = jnp.einsum(
        "csij,cjd->csid",
        picked,
        piece.reshape(blocks, tile, width),
        preferred_element_type=jnp.float32,
    )
    partial_rows = start_rows.at[targets.reshape(-1)].add(prod.reshape(-1, tile, width))
    partial_flat = partial_rows.reshape(row_blocks * tile, width)
    agg = lax.psum_scatter(
        partial_flat.astype(jnp.bfloat16), "rep", scatter_dimension=0, tiled=True
    )
    z = jnp.dot(features, w_self, preferred_element_type=jnp.float32) + jnp.dot(
        agg, w_neigh, preferred_element_type=jnp.float32
    )
    activations = jax.nn.silu(z).astype(jnp.bfloat16)
    sig = jax.nn.sigmoid(z)
    dz = (cotangent.astype(jnp.float32) * sig * (1.0 + z * (1.0 - sig))).astype(jnp.bfloat16)
    over_rows = (((0,), (0,)), ((), ()))
    over_cols = (((1,), (1,)), ((), ()))
    dagg = lax.dot_general(dz, w_neigh, over_cols, preferred_element_type=jnp.float32).astype(
        jnp.bfloat16
    )
    dagg_rows = lax.all_gather(dagg, "rep", axis=0, tiled=True)
    dagg_blocks = dagg_rows.reshape(row_blocks, tile, width)
    count = lax.axis_size("loop") * rows_dev
    picked, targets = tiles_for(count)
    grads = dagg_blocks[targets]
    neighbour_part = lax.psum_scatter(
        jnp.einsum("csij,csid->cjd", picked, grads, preferred_element_type=jnp.float32)
        .reshape(count, width)
        .astype(jnp.bfloat16),
        "loop",
        scatter_dimension=0,
        tiled=True,
    ).astype(jnp.float32)
    local_self = lax.dot_general(features, dz, over_rows, preferred_element_type=jnp.float32)
    local_neigh = lax.dot_general(agg, dz, over_rows, preferred_element_type=jnp.float32)
    sums = lax.psum((local_self, local_neigh), ("loop", "rep"))
    factor = 1.0 / math.sqrt(nodes)
    self_part = lax.dot_general(dz, w_self, over_cols, preferred_element_type=jnp.float32)
    grad_features = (self_part + neighbour_part).astype(jnp.bfloat16)
    return (activations, grad_features, sums[0] * factor, sums[1] * factor)


def solution(mesh):
    placed = (
        P(("loop", "rep"), None),
        P("loop", "rep", None, None, None),
        P("loop", "rep", None),
        P("loop", "rep"),
        P(),
        P(),
        P(("loop", "rep"), None),
    )
    return jax.shard_map(
        functools.partial(choose, mesh.shape["loop"], mesh.shape["rep"]),
        mesh=mesh,
        in_specs=placed,
        out_specs=(P(("loop", "rep"), None), P(("loop", "rep"), None), P(), P()),
        check_vma=False,
    )
```

```python
import functools
import math

import jax
import jax.numpy as jnp
from jax import lax
from jax.experimental import pallas as pl
from jax.experimental.pallas import tpu as pltpu
from jax.sharding import PartitionSpec as P

MESH = pl.DeviceIdType.MESH
HALVES = 2
SLAB_LIMIT = 8 * 1024 * 1024
OVER_ROWS = (((0,), (0,)), ((), ()))
OVER_COLS = (((1,), (1,)), ((), ()))


def mm(a, b, dims=(((1,), (0,)), ((), ()))):
    return lax.dot_general(a, b, dims, preferred_element_type=jnp.float32)


def loop(low, high, step):
    def one(k, carry):
        step(k)
        return carry

    lax.fori_loop(low, high, one, 0)


def kernel(
    nl, nr,
    f_hbm, adj_hbm, rows_ref, cnt_ref, ws_hbm, wn_hbm, ct_hbm,
    act_ref, gf_ref, gs_ref, gn_ref,
    f_ref, adj_ref, ws_ref, wn_ref, ct_ref, sem_in,
    dense, gat, acc, b1s, b1r, b2s, b2r, zf, fa, dz, dall,
    g1s, g1r, g32, g2s, g2r, g3f, g3s, g3r, gfin,
    f1s, f1r, ups, upr, dns, dnr, value, total,
    sem_au, sem_ad, sem_x, rec_a, sem_b1, rec_b1, sem_b2, rec_b2, sem_d, sem_ds, rec_d,
    sem_g1, rec_g1, sem_g2, rec_g2, sem_g3, rec_g3, sem_g4, rec_g4, sem_g5, rec_g5,
    sem_g6, rec_g6, sem_f1, rec_f1, sem_up, rec_up, sem_dn, rec_dn,
):
    nz, ny = nl // 2, nr // 2
    rows, width = f_ref.shape
    tile = adj_ref.shape[-1]
    slots = adj_ref.shape[2]
    half = rows // HALVES
    part = width // ny
    bf16, f32 = jnp.bfloat16, jnp.float32
    li, ri = lax.axis_index("loop"), lax.axis_index("rep")
    z, x = lax.div(li, 2), lax.rem(li, 2)
    y, c = lax.div(ri, 2), lax.rem(ri, 2)
    xp = z * 2 + 1 - x
    sib = y * 2 + 1 - c
    below, above = z > 0, z < nz - 1

    def zat(k):
        return lax.rem(z + k, nz)

    def yat(k):
        return lax.rem(y + k, ny)

    def lat(k):
        return lax.rem(li + k, nl)

    def rowsof(r):
        return pl.ds(pl.multiple_of(r * rows, rows), rows)

    def send(src, dst, s, r, lo, re):
        return pltpu.make_async_remote_copy(
            src_ref=src, dst_ref=dst, send_sem=s, recv_sem=r,
            device_id=(lo, re), device_id_type=MESH,
        )

    barrier = pltpu.get_barrier_semaphore()
    for k in range(1, nl):
        pl.semaphore_signal(barrier, inc=1, device_id=(lat(k), ri), device_id_type=MESH)
    for k in range(1, ny):
        pl.semaphore_signal(
            barrier, inc=1, device_id=(li, yat(k) * 2 + c), device_id_type=MESH
        )
    pl.semaphore_signal(barrier, inc=1, device_id=(li, sib), device_id_type=MESH)
    loads = [
        pltpu.make_async_copy(src, dst, sem_in.at[i])
        for i, (src, dst) in enumerate(
            ((f_hbm, f_ref), (adj_hbm, adj_ref), (ws_hbm, ws_ref), (wn_hbm, wn_ref), (ct_hbm, ct_ref))
        )
    ]
    for load in loads:
        load.start()
    loads[0].wait()
    pl.semaphore_wait(barrier, nl - 1 + ny)

    def block(p, h):
        at = pl.ds(h * half, half)
        return gat.at[p * 2 + x, at, :]

    def own(h):
        return f_ref.at[pl.ds(h * half, half), :]

    def send_x(p, h, src=None):
        at = block(p, h)
        return send(
            at if src is None else src, at, sem_x.at[p, h], rec_a.at[p * 2 + x, h], xp, ri
        )

    def send_au(p, h, src=None):
        at = block(p, h)
        return send(
            at if src is None else src, at, sem_au.at[p, h], rec_a.at[p * 2 + x, h],
            (z + 1) * 2 + x, ri,
        )

    def send_ad(p, h, src=None):
        at = block(p, h)
        return send(
            at if src is None else src, at, sem_ad.at[p, h], rec_a.at[p * 2 + x, h],
            (z - 1) * 2 + x, ri,
        )

    def got_a(j, h):
        at = gat.at[j, pl.ds(h * half, half), :]
        send(at, at, sem_x.at[0, 0], rec_a.at[j, h], xp, ri).wait_recv()

    for h in range(HALVES):
        @pl.when(above)
        def _():
            send_au(z, h, own(h)).start()

        @pl.when(below)
        def _():
            send_ad(z, h, own(h)).start()

        send_x(z, h, own(h)).start()

    for load in loads[1:]:
        load.wait()
    per = rows // tile
    row_blocks = nr * per

    def build(col):
        j, h = lax.div(col, per), lax.rem(col, per)
        cols = pl.ds(pl.multiple_of(h * tile, tile), tile)
        count = cnt_ref[0, col]
        places = [
            jnp.where(s < count, rows_ref[0, s, col], -1) for s in range(slots)
        ]

        for b in range(row_blocks):
            summed = jnp.zeros((tile, tile), f32)
            for s in range(slots):
                keep = jnp.where(places[s] == b, 1.0, 0.0).astype(f32)
                summed = summed + adj_ref[0, col, s].astype(f32) * keep
            dense[j, b * tile : (b + 1) * tile, cols] = summed.astype(bf16)

    loop(0, nl * per, build)
    zf[...] = mm(f_ref[...], ws_ref[...])
    fa[0] = f_ref[...]
    acc[...] = mm(dense[li], f_ref[...])

    for k in range(1, nz):
        for h in range(HALVES):
            @pl.when(z >= k)
            def _():
                got_a((z - k) * 2 + x, h)

                @pl.when(above)
                def _():
                    send_au(z - k, h).start()

                send_x(z - k, h).start()

            @pl.when(z + k < nz)
            def _():
                got_a((z + k) * 2 + x, h)

                @pl.when(below)
                def _():
                    send_ad(z + k, h).start()

                send_x(z + k, h).start()

    def column(k):
        j = zat(k) * 2 + x
        acc[...] += mm(dense[j], gat[j])

    loop(1, nz, column)

    def across(k):
        j = zat(k) * 2 + 1 - x
        for h in range(HALVES):
            got_a(j, h)
        acc[...] += mm(dense[j], gat[j])

    loop(0, nz, across)

    def send_b1(k):
        return send(b1s.at[k], b1r.at[k], sem_b1.at[k], rec_b1.at[k], li, sib)

    def send_b2(k):
        return send(
            b2s.at[k - 1], b2r.at[k - 1], sem_b2.at[k - 1], rec_b2.at[k - 1],
            li, yat(k) * 2 + c,
        )

    order = list(range(1, ny)) + [0]
    for k in order:
        b1s[k] = acc[rowsof(yat(k) * 2 + 1 - c), :].astype(bf16)
        send_b1(k).start()
    for k in order:
        send_b1(k).wait_recv()
        summed = acc[rowsof(yat(k) * 2 + c), :] + b1r[k].astype(f32)
        if k:
            b2s[k - 1] = summed.astype(bf16)
            send_b2(k).start()
        else:
            total[...] = summed
    for k in range(1, ny):
        send_b2(k).wait_recv()
        total[...] += b2r[k - 1].astype(f32)
    fa[1] = total[...].astype(bf16)

    zz = zf[...] + mm(fa[1], wn_ref[...])
    sig = jax.nn.sigmoid(zz)
    act_ref[...] = (zz * sig).astype(bf16)
    dz[...] = (ct_ref[...].astype(f32) * sig * (1.0 + zz * (1.0 - sig))).astype(bf16)
    dall[rowsof(ri), :] = mm(dz[...], wn_ref[...], OVER_COLS).astype(bf16)

    def send_d(k):
        at = dall.at[rowsof(ri)]
        return send(at, at, sem_d.at[k - 1], rec_d.at[ri], li, yat(k) * 2 + c)

    def send_ds(k):
        r = yat(k) * 2 + c
        at = dall.at[rowsof(r)]
        return send(at, at, sem_ds.at[k], rec_d.at[r], li, sib)

    def got_d(r):
        at = dall.at[rowsof(r)]
        send(at, at, sem_ds.at[0], rec_d.at[r], li, sib).wait_recv()

    for k in range(1, ny):
        send_d(k).start()
    send_ds(0).start()

    send_g1 = send(g1s, g1r, sem_g1, rec_g1, li, sib)
    g1s[...] = mm(fa[1 - c], dz[...], OVER_ROWS).astype(bf16)
    send_g1.start()
    g32[...] = mm(fa[c], dz[...], OVER_ROWS)
    for k in range(1, ny):
        got_d(yat(k) * 2 + c)
        send_ds(k).start()
    send_g1.wait_recv()
    g32[...] += g1r[...].astype(f32)

    def partof(yy):
        return pl.ds(pl.multiple_of(yy * part, part), part)

    def send_g2(k):
        return send(
            g2s.at[k - 1], g2r.at[k - 1], sem_g2.at[k - 1], rec_g2.at[k - 1],
            li, yat(k) * 2 + c,
        )

    for k in range(1, ny):
        g2s[k - 1] = g32[partof(yat(k)), :].astype(bf16)
        send_g2(k).start()
    for k in range(ny):
        got_d(yat(k) * 2 + 1 - c)

    def send_f1(d, h):
        return send(f1s.at[d, h], f1r.at[d, h], sem_f1.at[d, h], rec_f1.at[d, h], xp, ri)

    def send_up(d, h):
        return send(
            ups.at[d, h], upr.at[d, h], sem_up.at[d, h], rec_up.at[d, h], (z + 1) * 2 + x, ri
        )

    def send_dn(d, h):
        return send(
            dns.at[d, h], dnr.at[d, h], sem_dn.at[d, h], rec_dn.at[d, h], (z - 1) * 2 + x, ri
        )

    def away(d):
        product = mm(dense[d * 2 + 1 - x], dall[...], OVER_ROWS).astype(bf16)
        f1s[d] = product.reshape(HALVES, half, width)
        for h in range(HALVES):
            send_f1(d, h).start()

    def home(d, move, out, come, more):
        product = mm(dense[d * 2 + x], dall[...], OVER_ROWS)
        value[...] = product.reshape(HALVES, half, width)
        for h in range(HALVES):
            send_f1(d, h).wait_recv()
            value[h] += f1r[d, h].astype(f32)

            @pl.when(more)
            def _():
                move(d, h).wait_recv()
                value[h] += come[d, h].astype(f32)

            out[d, h] = value[h].astype(bf16)
            move(d, h).start()

    def sides(k, up, down):
        @pl.when(z + k < nz)
        def _():
            up(z + k)

        @pl.when(z >= k)
        def _():
            down(z - k)

    for k in range(nz - 1, nz // 2 - 1, -1):
        sides(k, away, away)

    def send_g3(k):
        return send(
            g3s.at[lat(k)], g3r.at[k - 1], sem_g3.at[k - 1], rec_g3.at[k - 1], lat(k), ri
        )

    mine = g32[partof(y), :]
    for k in range(1, ny):
        send_g2(k).wait_recv()
        mine = mine + g2r[k - 1].astype(f32)
    g3f[...] = mine.reshape(g3f.shape)
    g3s[...] = g3f[...].astype(bf16)
    for k in range(1, nl):
        send_g3(k).start()

    for k in range(nz // 2 - 1, 0, -1):
        sides(k, away, away)
    away(z)

    def home_up(d):
        home(d, send_up, ups, upr, below)

    def home_down(d):
        home(d, send_dn, dns, dnr, above)

    for k in range(nz - 1, nz // 2 - 1, -1):
        sides(k, home_up, home_down)

    def send_g4(k):
        at = gfin.at[c, y, li]
        return send(at, at, sem_g4.at[k - 1], rec_g4.at[li], lat(k), ri)

    small = g3f[li]
    for k in range(1, nl):
        send_g3(k).wait_recv()
        small = small + g3r[k - 1].astype(f32)
    gfin[c, y, li] = small.astype(bf16)
    for k in range(1, nl):
        send_g4(k).start()
    for k in range(nz // 2 - 1, 0, -1):
        sides(k, home_up, home_down)
    total[...] = mm(dz[...], ws_ref[...], OVER_COLS) + mm(
        dense[li], dall[...], OVER_ROWS
    )
    def send_g5(k, p):
        at = gfin.at[c, y, p]
        return send(
            at, at, sem_g5.at[k - 1, p], rec_g5.at[y, p], li, yat(k) * 2 + c
        )

    def send_g6(k, p):
        at = gfin.at[c, yat(k), p]
        return send(at, at, sem_g6.at[k, p], rec_g6.at[yat(k), p], li, sib)

    for i in range(nl):
        p = lat(i)
        if i:
            at = gfin.at[c, y, p]
            send(at, at, sem_g4.at[0], rec_g4.at[p], p, ri).wait_recv()
        for k in range(1, ny):
            send_g5(k, p).start()
        send_g6(0, p).start()
    for k in range(1, ny):
        for i in range(nl):
            p = lat(i)
            at = gfin.at[c, yat(k), p]
            send(
                at, at, sem_g5.at[0, p], rec_g5.at[yat(k), p], li, yat(k) * 2 + c
            ).wait_recv()
            send_g6(k, p).start()
    for h in range(HALVES):
        at = slice(h * half, (h + 1) * half)
        send_f1(z, h).wait_recv()
        total[at] += f1r[z, h].astype(f32)

        @pl.when(below)
        def _():
            send_up(z, h).wait_recv()
            total[at] += upr[z, h].astype(f32)

        @pl.when(above)
        def _():
            send_dn(z, h).wait_recv()
            total[at] += dnr[z, h].astype(f32)

    gf_ref[...] = total[...].astype(bf16)
    for k in range(ny):
        for p in range(nl):
            at = gfin.at[1 - c, yat(k), p]
            send(at, at, sem_g6.at[0, p], rec_g6.at[yat(k), p], li, sib).wait_recv()
    gs_ref[...] = gfin[0].reshape(width, width)
    gn_ref[...] = gfin[1].reshape(width, width)

    for h in range(HALVES):
        for p in range(nz):
            send_x(p, h).wait_send()
            send_f1(p, h).wait_send()

            @pl.when(above & (p <= z))
            def _():
                send_au(p, h).wait_send()

            @pl.when(below & (p >= z))
            def _():
                send_ad(p, h).wait_send()

            @pl.when(p > z)
            def _():
                send_up(p, h).wait_send()

            @pl.when(p < z)
            def _():
                send_dn(p, h).wait_send()

    for k in range(ny):
        send_b1(k).wait_send()
        send_ds(k).wait_send()
        for p in range(nl):
            send_g6(k, p).wait_send()
    for k in range(1, ny):
        send_b2(k).wait_send()
        send_d(k).wait_send()
        send_g2(k).wait_send()
        for p in range(nl):
            send_g5(k, p).wait_send()
    send_g1.wait_send()
    for k in range(1, nl):
        send_g3(k).wait_send()
        send_g4(k).wait_send()


def fused(nl, nr, features, adj_values, adj_rows, slot_counts, w_self, w_neigh, cotangent):
    rows, width = features.shape
    bf16, f32 = jnp.bfloat16, jnp.float32
    nz, ny = nl // 2, nr // 2
    part = width // ny
    q = part // nl
    scale = 1.0 / math.sqrt(rows * nl * nr)
    vm = pl.BlockSpec(memory_space=pltpu.VMEM)
    sm = pl.BlockSpec(memory_space=pltpu.SMEM)
    hbm = pl.BlockSpec(memory_space=pl.ANY)
    half = rows // HALVES

    def buf(*shape):
        return pltpu.VMEM(shape, bf16)

    def wide(*shape):
        return pltpu.VMEM(shape, f32)

    def dma(*shape):
        return pltpu.SemaphoreType.DMA(shape)

    out = pl.pallas_call(
        functools.partial(kernel, nl, nr),
        out_shape=(
            jax.ShapeDtypeStruct((rows, width), bf16),
            jax.ShapeDtypeStruct((rows, width), bf16),
            jax.ShapeDtypeStruct((width, width), bf16),
            jax.ShapeDtypeStruct((width, width), bf16),
        ),
        in_specs=[hbm, hbm, sm, sm, hbm, hbm, hbm],
        out_specs=(vm, vm, vm, vm),
        scratch_shapes=[
            buf(rows, width), buf(*adj_values.shape), buf(width, width), buf(width, width),
            buf(rows, width), dma(5),
            buf(nl, nr * rows, rows), buf(nl, rows, width), wide(nr * rows, width),
            buf(ny, rows, width), buf(ny, rows, width),
            buf(ny - 1, rows, width), buf(ny - 1, rows, width),
            wide(rows, width), buf(2, rows, width), buf(rows, width), buf(nr * rows, width),
            buf(width, width), buf(width, width), wide(width, width),
            buf(ny - 1, part, width), buf(ny - 1, part, width),
            wide(nl, q, width), buf(nl, q, width), buf(nl - 1, q, width),
            buf(2, ny, nl, q, width),
            *[buf(nz, HALVES, half, width) for _ in range(6)],
            wide(HALVES, half, width), wide(rows, width),
            dma(nz, HALVES), dma(nz, HALVES), dma(nz, HALVES), dma(nl, HALVES), dma(ny), dma(ny), dma(ny - 1), dma(ny - 1),
            dma(ny - 1), dma(ny), dma(nr),
            pltpu.SemaphoreType.DMA, pltpu.SemaphoreType.DMA, dma(ny - 1), dma(ny - 1),
            dma(nl - 1), dma(nl - 1), dma(nl - 1), dma(nl), dma(ny - 1, nl), dma(ny, nl),
            dma(ny, nl), dma(ny, nl), *[dma(nz, HALVES) for _ in range(6)],
        ],
        compiler_params=pltpu.CompilerParams(
            collective_id=0, has_side_effects=True, vmem_limit_bytes=60 * 1024 * 1024
        ),
    )(features, adj_values, jnp.swapaxes(adj_rows, 1, 2), slot_counts, w_self, w_neigh, cotangent)
    return (out[0], out[1], out[2].astype(f32) * scale, out[3].astype(f32) * scale)


def choose(nl, nr, features, *rest):
    rows = features.shape[0]
    if nl * nr * rows * rows * 2 > SLAB_LIMIT:
        return body(features, *rest)
    return fused(nl, nr, features, *rest)


def body(features, adj_values, adj_rows, slot_counts, w_self, w_neigh, cotangent):
    rows_dev, width = features.shape
    tile = adj_values.shape[-1]
    nodes = rows_dev * lax.axis_size("loop") * lax.axis_size("rep")
    row_blocks = lax.axis_size("rep") * rows_dev // tile
    live = lax.broadcasted_iota(jnp.int32, adj_rows.shape[1:], 1) < slot_counts[0][:, None]
    tiles_live = adj_values[0] * live.astype(jnp.bfloat16)[:, :, None, None]
    block_rows = adj_rows[0]

    def tiles_for(count):
        blocks = count // tile
        return (tiles_live, block_rows)

    start_rows = jnp.zeros((row_blocks, tile, width), jnp.float32)
    piece = lax.all_gather(features, "loop", axis=0, tiled=True)
    blocks = piece.shape[0] // tile
    picked, targets = tiles_for(piece.shape[0])
    prod = jnp.einsum(
        "csij,cjd->csid",
        picked,
        piece.reshape(blocks, tile, width),
        preferred_element_type=jnp.float32,
    )
    partial_rows = start_rows.at[targets.reshape(-1)].add(prod.reshape(-1, tile, width))
    partial_flat = partial_rows.reshape(row_blocks * tile, width)
    agg = lax.psum_scatter(
        partial_flat.astype(jnp.bfloat16), "rep", scatter_dimension=0, tiled=True
    )
    z = jnp.dot(features, w_self, preferred_element_type=jnp.float32) + jnp.dot(
        agg, w_neigh, preferred_element_type=jnp.float32
    )
    activations = jax.nn.silu(z).astype(jnp.bfloat16)
    sig = jax.nn.sigmoid(z)
    dz = (cotangent.astype(jnp.float32) * sig * (1.0 + z * (1.0 - sig))).astype(jnp.bfloat16)
    over_rows = (((0,), (0,)), ((), ()))
    over_cols = (((1,), (1,)), ((), ()))
    dagg = lax.dot_general(dz, w_neigh, over_cols, preferred_element_type=jnp.float32).astype(
        jnp.bfloat16
    )
    dagg_rows = lax.all_gather(dagg, "rep", axis=0, tiled=True)
    dagg_blocks = dagg_rows.reshape(row_blocks, tile, width)
    count = lax.axis_size("loop") * rows_dev
    picked, targets = tiles_for(count)
    grads = dagg_blocks[targets]
    neighbour_part = lax.psum_scatter(
        jnp.einsum("csij,csid->cjd", picked, grads, preferred_element_type=jnp.float32)
        .reshape(count, width)
        .astype(jnp.bfloat16),
        "loop",
        scatter_dimension=0,
        tiled=True,
    ).astype(jnp.float32)
    local_self = lax.dot_general(features, dz, over_rows, preferred_element_type=jnp.float32)
    local_neigh = lax.dot_general(agg, dz, over_rows, preferred_element_type=jnp.float32)
    sums = lax.psum((local_self, local_neigh), ("loop", "rep"))
    factor = 1.0 / math.sqrt(nodes)
    self_part = lax.dot_general(dz, w_self, over_cols, preferred_element_type=jnp.float32)
    grad_features = (self_part + neighbour_part).astype(jnp.bfloat16)
    return (activations, grad_features, sums[0] * factor, sums[1] * factor)


def solution(mesh):
    placed = (
        P(("loop", "rep"), None),
        P("loop", "rep", None, None, None),
        P("loop", "rep", None),
        P("loop", "rep"),
        P(),
        P(),
        P(("loop", "rep"), None),
    )
    return jax.shard_map(
        functools.partial(choose, mesh.shape["loop"], mesh.shape["rep"]),
        mesh=mesh,
        in_specs=placed,
        out_specs=(P(("loop", "rep"), None), P(("loop", "rep"), None), P(), P()),
        check_vma=False,
    )
```
